32 devices in a mesh: rotor: 4 (over y, core), blk: 8 (over z, x).
Axes of the slice: x: 2, y: 2, z: 4, core: 2. Of those that a mesh axis runs over, the one named last changes fastest.
Arguments:
- positions: float32 [3, 131072], P(None, ('rotor', 'blk')), may hold values from -6 to 6
- strengths: float32 [3, 131072], P(None, ('rotor', 'blk'))
- blade_of_block: int32 [1024], P(('rotor', 'blk')), may hold values from 0 to 29
- circulation: float32 [30], replicated, may hold values from 0.5 to 2
- tile_source_dev: int32 [8192, 1], P(('rotor', 'blk')), may hold values from 0 to 31; in each aligned block of 256 rows (0 to 255, 256 to 511, ...) at most 12 rows name the same one
- tile_source_blk: int32 [8192], P(('rotor', 'blk')), may hold values from 0 to 31
- tile_target: int32 [8192], P(('rotor', 'blk')), may hold values from 0 to 31
- tile_count: int32 [32], P(('rotor', 'blk')), may hold values from 128 to 256, as said below
Outputs:
- velocity: float32 [3, 131072], P(None, ('rotor', 'blk'))
- strength_rate: float32 [3, 131072], P(None, ('rotor', 'blk'))
The draws below stay inside these ranges and needn't reach their ends.
Inputs may be any that keep to these rules, and one draw needn't show every extreme that they name: `tile_source_dev`: among the 256 slots of one device no device number appears more than 12 times, and one appears exactly 12 times. `tile_count`: some device has all 256 slots live.
All inputs are finite; a program needn't handle non-finite values.
Results may differ from the reference program's by a relative error of at most 0.0003.
Values sent between devices are 32-bit elements; how exact they have to be, the bound alone decides.
A program may use at most 128 MiB of HBM per device.

```python
import math
import jax
import jax.numpy as jnp
import numpy as np
from jax import lax

PB = 128
NB = 32
CAP = 256
BLADES = 30
NDEV = 32
SLOT = 12
NBLK = 1024
NPART = 131072
NTILES = 8192
N_ROTOR = 4
N_BLK = 8


def draw_strengths(key, part):
    position_frac = jnp.arange(NPART, dtype=jnp.float32) / (NPART - 1)
    ramp_scale = 1.0 + 2.0 * position_frac
    values = jnp.clip(jax.random.normal(key, (3, NPART), jnp.float32), -6.0, 6.0)
    return values * ramp_scale[None, :]


def draw_tile_count(key, part):
    counts = jax.random.randint(key, (NDEV,), CAP // 2, CAP + 1)
    fullest = jax.random.randint(jax.random.fold_in(key, 1), (), 0, NDEV)
    return counts.at[fullest].set(CAP).astype(jnp.int32)


def touch_ends(values, rng, least, high):
    longest = values.shape.index(max(values.shape))
    spots = []
    for shift in (0, 1):
        where = [jax.random.randint(jax.random.fold_in(rng, axis), (), 0, length) for axis, length in enumerate(values.shape)]
        where[longest] = (where[longest] + shift) % values.shape[longest]
        spots.append(tuple(where))
    return values.at[spots[0]].set(least).at[spots[1]].set(high)


def levels(stream_key, extent, shards, smallest, top_value):
    factor_of = 1.0
    for axis_at, blocks in shards:
        draws = jax.random.uniform(jax.random.fold_in(jax.random.fold_in(stream_key, 6), axis_at), (blocks,), jnp.float32, smallest / len(shards), top_value / len(shards))
        factor_of = factor_of * jnp.repeat(jnp.exp(draws), extent[axis_at] // blocks).reshape((-1,) + (1,) * (len(extent) - 1 - axis_at))
    return factor_of


def assign_block(rng, own, number, rows, amount, top, reach, skew):
    ranking = jax.random.permutation(rng, amount)
    crowded, common = shares(amount, rows * top, reach, skew, True), shares(amount, rows * top, reach, skew, False)
    places = jnp.arange(amount)

    def named(sizes, rotation):
        used = int((sizes > 0).sum())
        fixed = max(1, used // 4)
        passed = fixed + (places - fixed + rotation * (used - fixed)) % max(1, amount - fixed)
        return jnp.zeros((amount,), jnp.int32).at[ranking[jnp.where(places < fixed, places, passed)]].set(jnp.asarray(sizes, jnp.int32))

    sizes = jnp.where(number % 4 == 0, named(crowded, number // 4), named(common, number - number // 4 - 1))
    mixed = jax.random.permutation(jax.random.fold_in(own, 3), amount)
    donor, sink = mixed[0:amount // 2 * 2:2], mixed[1:amount // 2 * 2:2]
    room = jnp.minimum(sizes[donor] - 1, reach - sizes[sink]) // 2
    room = jnp.where((donor == ranking[0]) | (sink == ranking[0]) | (sizes[sink] == 0), 0, jnp.maximum(room, 0))
    passed = jax.random.randint(jax.random.fold_in(own, 4), (amount // 2,), 0, 1 << 20) % (room + 1)
    sizes = sizes.at[donor].add(-passed).at[sink].add(passed)
    members = jnp.searchsorted(jnp.cumsum(sizes), jnp.arange(rows * top), side="right").astype(jnp.int32)
    listing = members.reshape(top, rows).T
    listing = listing[jax.random.permutation(jax.random.fold_in(own, 1), rows)]
    rotation = jax.random.randint(jax.random.fold_in(own, 2), (rows, 1), 0, top)
    return jnp.take_along_axis(listing, (jnp.arange(top)[None, :] + rotation) % top, axis=1)


def shares(amount, total, limit, slope, full):
    weights = [(1 << 20) // math.isqrt(grade ** slope) + 1 for grade in range(1, amount + 1)]
    largest = limit if full else min(limit, max(-(-total // amount), total * weights[0] // sum(weights)))
    least = 1 if total - largest >= amount - 1 else 0
    given, rest = [largest] + [least] * (amount - 1), total - largest - least * (amount - 1)
    while rest > 0:
        movable = [i for i in range(1, amount) if given[i] < largest] or [i for i in range(1, amount) if given[i] < limit]
        pool, remaining = sum([weights[i] for i in movable]), rest
        for i in movable:
            extra = min(limit - given[i], max(1, remaining * weights[i] // pool), rest)
            given[i] = given[i] + extra
            rest = rest - extra
    return np.array(given)


def centred(rng, shape, width, bound, shards=(), held_as=jnp.bfloat16):
    result = width * jax.random.normal(rng, shape, jnp.float32)
    if shards:
        result = result * levels(rng, shape, shards, -0.22, 0.18)
    return jnp.clip(result, -bound, bound).astype(held_as)


def setup_inputs(seed: int = 0) -> dict:
    key_list = jax.random.split(jax.random.key(seed), 9)
    positions = centred(key_list[0], (3, NPART), 1.0, 6.0, ((1, 32),), jnp.float32)
    strengths = draw_strengths(jax.random.fold_in(key_list[8], 71), 0)
    blade_of_block = touch_ends(jax.random.randint(key_list[2], (NBLK,), 0, BLADES), jax.random.fold_in(key_list[2], 1), 0, BLADES - 1).astype(jnp.int32)
    circulation = jnp.clip(jnp.exp(jax.random.uniform(key_list[3], (BLADES,), jnp.float32, math.log(0.5), math.log(2.0))), 0.5, 2.0)
    tile_source_dev_keys = jax.random.split(jax.random.fold_in(key_list[4], 1), NTILES // CAP)
    tile_source_dev_turns = jax.random.permutation(jax.random.fold_in(key_list[4], 3), NTILES // CAP)
    tile_source_dev = jax.vmap(lambda own, number: assign_block(jax.random.fold_in(key_list[4], 2), own, number, CAP, NDEV, 1, SLOT, 2))(tile_source_dev_keys, tile_source_dev_turns).reshape((NTILES, 1))
    tile_source_blk = touch_ends(jax.random.randint(key_list[5], (NTILES,), 0, NB), jax.random.fold_in(key_list[5], 1), 0, NB - 1).astype(jnp.int32)
    tile_target = touch_ends(jax.random.randint(key_list[6], (NTILES,), 0, NB), jax.random.fold_in(key_list[6], 1), 0, NB - 1).astype(jnp.int32)
    tile_count = draw_tile_count(jax.random.fold_in(key_list[8], 71), 0)
    return dict(positions=positions, strengths=strengths, blade_of_block=blade_of_block, circulation=circulation, tile_source_dev=tile_source_dev, tile_source_blk=tile_source_blk, tile_target=tile_target, tile_count=tile_count)


inverse_four_pi = 1.0 / (4.0 * math.pi)
core_square = 1.0
diffusion_rate = 2.0
highest = lax.Precision.HIGHEST

def cross_rows(left, right):
    return jnp.stack([left[1] * right[2] - left[2] * right[1], left[2] * right[0] - left[0] * right[2], left[0] * right[1] - left[1] * right[0]])

def contract(matrix, values):
    return jnp.einsum('ts,cs->ct', matrix, values, precision=highest)

def kernels(target_pos, source_pos):
    offset_vec = target_pos[:, :, None] - source_pos[:, None, :]
    distance_sq = lax.optimization_barrier(jnp.sum(offset_vec * offset_vec, axis=0))
    inverse = 1.0 / (distance_sq + core_square)
    green_kernel = inverse_four_pi * inverse * jnp.sqrt(inverse)
    return (green_kernel, 3.0 * green_kernel * inverse, jnp.exp(-distance_sq / core_square))

def toward(target, source, green_kernel, hessian, smooth):
    target_pos, target_str = (target[:3], target[3:])
    source_pos, source_str = (source[:3], source[3:])
    spin_src = cross_rows(source_pos, source_str)
    green_str = contract(green_kernel, source_str)
    velocity = contract(green_kernel, spin_src) - cross_rows(target_pos, green_str)
    along_axis = lax.optimization_barrier(jnp.sum(target_str * target_pos, axis=0))[:, None] - jnp.einsum('ct,cs->ts', target_str, source_pos, precision=highest)
    lever_arm = hessian * along_axis
    stretch = cross_rows(target_pos, contract(lever_arm, source_str)) - contract(lever_arm, spin_src) - cross_rows(target_str, green_str)
    diffusion = contract(smooth, source_str) - lax.optimization_barrier(jnp.sum(smooth, axis=1))[None, :] * target_str
    return jnp.concatenate([velocity, stretch + diffusion_rate * diffusion], axis=0)

def near_block(target, sources, validity):
    green_kernel, hessian, smooth = kernels(target[:3], sources[:3])
    return toward(target, sources, green_kernel, hessian, smooth * validity[None, :])

def tile_pair(target, source):
    green_kernel, hessian, smooth = kernels(target[:3], source[:3])
    forward = toward(target, source, green_kernel, hessian, smooth)
    backward = toward(source, target, green_kernel.T, hessian.T, smooth.T)
    return (forward, backward)

def reference(positions, strengths, blade_of_block, circulation, tile_source_dev, tile_source_blk, tile_target, tile_count):
    nblocks = blade_of_block.shape[0]
    magnitude = jnp.sqrt(lax.optimization_barrier(jnp.sum(strengths * strengths, axis=0))).reshape(nblocks, PB).sum(axis=1)
    member = (blade_of_block[:, None] == jnp.arange(BLADES, dtype=jnp.int32)[None, :]).astype(jnp.float32)
    totals = lax.optimization_barrier(jnp.sum(member * magnitude[:, None], axis=0))
    counted = lax.optimization_barrier(jnp.sum(member, axis=0)) * PB
    factor = circulation / (totals / jnp.maximum(counted, 1.0) + 1e-06)
    block_factor = lax.optimization_barrier(jnp.sum(member * factor[None, :], axis=1))
    scaled = strengths * jnp.repeat(block_factor, PB)[None, :]
    blocks = jnp.concatenate([positions, scaled], axis=0).reshape(6, nblocks, PB).transpose(1, 0, 2)
    seq_len = N_BLK * NB
    chains = blocks.reshape(N_ROTOR, seq_len, 6, PB)
    padded = jnp.pad(chains, ((0, 0), (1, 1), (0, 0), (0, 0)))
    zero_idx = jnp.zeros((), jnp.int32)

    def near_one(index):
        rotor_id = (index // seq_len).astype(jnp.int32)
        place = (index % seq_len).astype(jnp.int32)
        window = lax.dynamic_slice(padded, (rotor_id, place, zero_idx, zero_idx), (1, 3, 6, PB))[0]
        sources = window.transpose(1, 0, 2).reshape(6, 3 * PB)
        validity = jnp.concatenate([jnp.full((PB,), place > 0), jnp.ones((PB,), bool), jnp.full((PB,), place < seq_len - 1)]).astype(jnp.float32)
        return near_block(blocks[index], sources, validity)
    near = lax.map(jax.vmap(near_one), jnp.arange(nblocks, dtype=jnp.int32).reshape(-1, 16))
    near = near.reshape(nblocks, 6, PB)
    ntiles = tile_target.shape[0]
    slot_ids = jnp.arange(ntiles, dtype=jnp.int32)
    owner = slot_ids // CAP
    target_ids = owner * NB + tile_target
    source_ids = tile_source_dev[:, 0] * NB + tile_source_blk
    live_tile = (slot_ids % CAP < tile_count[owner]).astype(jnp.float32)

    def step(accumulated, group):
        target_group, source_group, alive_mask = group
        target_out, source_out = jax.vmap(tile_pair)(blocks[target_group], blocks[source_group])
        accumulated = accumulated.at[target_group].add(target_out * alive_mask[:, None, None])
        accumulated = accumulated.at[source_group].add(source_out * alive_mask[:, None, None])
        return (accumulated, None)
    total, _ = lax.scan(step, near, (target_ids.reshape(-1, 16), source_ids.reshape(-1, 16), live_tile.reshape(-1, 16)))
    flat_terms = total.transpose(1, 0, 2).reshape(6, nblocks * PB)
    return (flat_terms[:3], flat_terms[3:])
```

```python
import functools
import math

import jax
import jax.numpy as jnp
from jax import lax
from jax.experimental import pallas as pl
from jax.experimental.pallas import tpu as pltpu
from jax.sharding import PartitionSpec as P

AXES = ("rotor", "blk")
green_scale = 1.0 / (4.0 * math.pi)
smooth_scale = 2.0 * math.e
log2_e = math.log2(math.e)
ROWS = 8
f32, bf16 = jnp.float32, jnp.bfloat16


def split3(v):
    hi = v.astype(bf16)
    rest = v - hi.astype(f32)
    mid = rest.astype(bf16)
    return hi, mid, (rest - mid.astype(f32)).astype(bf16)


def split2(v):
    hi = v.astype(bf16)
    return hi, (v - hi.astype(f32)).astype(bf16)


def roll(v, up):
    return pltpu.roll(v, (ROWS - up) % ROWS, 0)


def row_ids(width):
    return lax.broadcasted_iota(jnp.int32, (ROWS, width), 0)


def features(raw, factor):
    row = row_ids(raw.shape[1])
    is_str = ((row >= 3) & (row < 6)) | (row == 7)
    base = jnp.where(is_str, raw * factor, raw)
    xx = jnp.where(row < 3, base, roll(base, 5))
    aa = jnp.where(row < 3, roll(base, 3), base)
    x1, x2, a1, a2 = roll(xx, 1), roll(xx, 2), roll(aa, 1), roll(aa, 2)
    spin = jnp.where(row < 3, x1 * a2 - x2 * a1, 0.0)
    group = jnp.where(row < 5, aa, jnp.where(row == 5, 1.0, 0.0))
    hi, lo = split2(jnp.concatenate([group, spin], axis=0))
    values = jnp.concatenate([hi, lo], axis=0)
    return base, values, (x1, x2, a1, a2, aa)


def source_front(base):
    row = row_ids(base.shape[1])
    full = jnp.concatenate([base, jnp.where(row == 0, 1.0, 0.0)], axis=0)
    hi, mid, lo = split3(full)
    return jnp.concatenate([hi, hi, mid, mid, hi, lo], axis=0)


def target_front(base):
    row = row_ids(base.shape[1])
    norm, along = base[6:7], base[7:8]
    zero = jnp.zeros_like(base)
    dist = jnp.concatenate(
        [
            jnp.where(row < 3, -2.0 * base, jnp.where(row == 6, 1.0, 0.0)),
            jnp.where(row == 0, norm + 1.0, zero),
        ],
        axis=0,
    )
    to_target = jnp.concatenate(
        [jnp.where(row < 3, -roll(base, 3), 0.0), jnp.where(row == 0, along, zero)], axis=0
    )
    shifted = roll(base, 5)
    to_source = jnp.concatenate(
        [
            jnp.where((row >= 3) & (row < 6), -shifted, jnp.where(row == 7, 1.0, 0.0)),
            zero,
        ],
        axis=0,
    )
    hi, mid, lo = split3(jnp.concatenate([dist, to_target, to_source], axis=1))
    return jnp.concatenate([hi, mid, hi, mid, lo, hi], axis=0)


def combine(sums, own):
    width = sums.shape[1] // 3
    x1, x2, a1, a2, aa = own
    half = sums.shape[0] // 2
    sums = sums[:half] + sums[half:]
    ga, la, ea = (sums[:ROWS, i * width : (i + 1) * width] for i in range(3))
    gs, ls = (sums[ROWS:, i * width : (i + 1) * width] for i in range(2))
    ga1, ga2, la1, la2 = roll(ga, 1), roll(ga, 2), roll(la, 1), roll(la, 2)
    u = green_scale * (gs - (x1 * ga2 - x2 * ga1))
    w = (
        (3.0 * green_scale) * (x1 * la2 - x2 * la1 - ls)
        - green_scale * (a1 * ga2 - a2 * ga1)
        + smooth_scale * (ea - ea[5:6] * aa)
    )
    return jnp.where(row_ids(width) < 4, u, roll(w, 4))


def pair(front_s, values_s, own_s, front_t, values_t, own_t, both):
    width = values_s.shape[1]
    d = lax.dot_general(
        front_s, front_t, (((0,), (0,)), ((), ())), preferred_element_type=f32
    )
    p = d[:, :width]
    inv = lax.rsqrt(p)
    inv2 = inv * inv
    g = inv2 * inv
    h = g * inv2
    e = jnp.exp2(p * (-log2_e))
    g2, e2 = split2(g), split2(e)
    l2 = split2(h * d[:, width : 2 * width])
    ahead = jnp.concatenate(
        [jnp.concatenate([g2[i], l2[i], e2[i]], axis=1) for i in range(2)], axis=0
    )
    lhs = jnp.concatenate([values_s, values_s], axis=1)
    to_t = combine(jnp.dot(lhs, ahead, preferred_element_type=f32), own_t)
    if not both:
        return to_t, None
    m2 = split2(h * d[:, 2 * width :])
    back = jnp.concatenate(
        [jnp.concatenate([v[0], v[1]], axis=1) for v in (g2, m2, e2)], axis=0
    )
    lhs = jnp.concatenate([values_t, values_t], axis=1)
    sums = lax.dot_general(lhs, back, (((1,), (1,)), ((), ())), preferred_element_type=f32)
    return to_t, combine(sums, own_s)


def prepare(state, factor_of, front, values, own, sources=None):
    def step(k, carry):
        base, vals, perm = features(state[k], factor_of(k))
        front[k] = target_front(base)
        values[k] = vals
        for i, v in enumerate(perm):
            own[k, i] = v
        if sources is not None:
            sources[k] = source_front(base)
        return carry

    lax.fori_loop(0, state.shape[0], step, 0)


def near_kernel(factor, state, out, front, values, own, sources):
    prepare(state, lambda k: factor[k], front, values, own, sources)
    blocks = state.shape[0]

    def held(k):
        return values[k], tuple(own[k, i] for i in range(5))

    def alone(k, carry):
        v, o = held(k)
        out[k] = pair(sources[k], v, o, front[k], v, o, False)[0]
        return carry

    lax.fori_loop(0, blocks, alone, 0)

    def chain(k, carry):
        vs, os = held(k + 1)
        vt, ot = held(k)
        to_t, to_s = pair(sources[k + 1], vs, os, front[k], vt, ot, True)
        out[k] += to_t
        out[k + 1] += to_s
        return carry

    lax.fori_loop(0, blocks - 1, chain, 0)


def tile_kernel(live, target, source, factor, first, state, near, acc, dense, front, values, own):
    mine = acc.shape[0]
    prepare(near.at[1], lambda k: factor[first[0] + k], front, values, own)

    def clear(k, carry):
        dense[pl.ds(k * 16, 16)] = jnp.zeros((16,) + dense.shape[1:], f32)
        return carry

    lax.fori_loop(0, dense.shape[0] // 16, clear, 0)

    def start(k, carry):
        acc[k] = near[0, k]
        return carry

    lax.fori_loop(0, mine, start, 0)

    def one(c):
        t, s = target[c], source[c]
        base, vs, os = features(state[s], factor[s])
        vt, ot = values[t], tuple(own[t, i] for i in range(5))
        return t, s, pair(source_front(base), vs, os, front[t], vt, ot, True)

    def add(t, s, terms):
        acc[t] += terms[0]
        dense[s] += terms[1]

    count = live[0]

    def step(c, carry):
        add(*one(c))
        return carry

    def two(c, carry):
        first_one, second_one = one(2 * c), one(2 * c + 1)
        add(*first_one)
        add(*second_one)
        return carry

    lax.fori_loop(0, count // 2, two, 0)
    lax.fori_loop(count // 2 * 2, count, step, 0)


def scratch(blocks, width):
    return [
        pltpu.VMEM((blocks, 96, 3 * width), bf16),
        pltpu.VMEM((blocks, 32, width), bf16),
        pltpu.VMEM((blocks, 5, ROWS, width), f32),
    ]


smem = pl.BlockSpec(memory_space=pltpu.SMEM)
vmem = pl.BlockSpec(memory_space=pltpu.VMEM)


def near_field(factor, state):
    blocks, _, width = state.shape
    return pl.pallas_call(
        near_kernel,
        out_shape=jax.ShapeDtypeStruct(state.shape, f32),
        in_specs=[smem, vmem],
        out_specs=vmem,
        scratch_shapes=scratch(blocks, width) + [pltpu.VMEM((blocks, 96, width), bf16)],
        compiler_params=pltpu.CompilerParams(vmem_limit_bytes=24 * 2**20),
        cost_estimate=pl.CostEstimate(
            flops=blocks * width * width * 400, bytes_accessed=2**20, transcendentals=0
        ),
    )(factor, state)


def tiles(live, target, source, factor, first, state, near):
    blocks, width = near.shape[1], near.shape[3]
    return pl.pallas_call(
        tile_kernel,
        out_shape=(
            jax.ShapeDtypeStruct(near.shape[1:], f32),
            jax.ShapeDtypeStruct(state.shape, f32),
        ),
        in_specs=[smem] * 5 + [vmem] * 2,
        out_specs=(vmem, vmem),
        scratch_shapes=scratch(blocks, width),
        compiler_params=pltpu.CompilerParams(vmem_limit_bytes=48 * 2**20),
    )(live, target, source, factor, first, state, near)


def local(
    positions,
    strengths,
    blade_of_block,
    circulation,
    tile_source_dev,
    tile_source_blk,
    tile_target,
    tile_count,
):
    blocks = blade_of_block.shape[0]
    width = positions.shape[1] // blocks
    n_blk = lax.axis_size("blk")
    place = lax.axis_index("blk")
    me = lax.axis_index("rotor") * n_blk + place

    magnitude = jnp.sqrt(jnp.sum(strengths * strengths, axis=0)).reshape(blocks, width).sum(axis=1)
    facts = jnp.concatenate([magnitude, blade_of_block.astype(f32)]).reshape(1, -1)
    state = jnp.concatenate(
        [
            positions,
            strengths,
            jnp.sum(positions * positions, axis=0, keepdims=True),
            jnp.sum(positions * strengths, axis=0, keepdims=True),
        ],
        axis=0,
    )
    state = state.reshape(ROWS, blocks, width).transpose(1, 0, 2)
    every_fact = lax.all_gather(facts, AXES, axis=0, tiled=True)
    everyone = lax.all_gather(state, AXES, axis=0, tiled=True)

    member = (
        every_fact[:, blocks:].reshape(-1, 1)
        == jnp.arange(circulation.shape[0], dtype=jnp.int32).astype(f32)[None, :]
    ).astype(f32)
    totals = jnp.sum(member * every_fact[:, :blocks].reshape(-1, 1), axis=0)
    counted = jnp.sum(member, axis=0) * width
    blade_factor = circulation / (totals / jnp.maximum(counted, 1.0) + 1e-06)
    factor = jnp.sum(member * blade_factor[None, :], axis=1)
    own_factor = lax.dynamic_slice_in_dim(factor, me * blocks, blocks)
    near = near_field(own_factor, state)

    has_next = (place < n_blk - 1).astype(jnp.int32)
    source = tile_source_dev[:, 0] * blocks + tile_source_blk
    total = lax.axis_size("rotor") * n_blk * blocks
    edge_source = jnp.minimum((me + 1) * blocks, total - 1)
    target = jnp.concatenate([tile_target, jnp.zeros((1,), jnp.int32)])
    source = jnp.concatenate([source, jnp.zeros((1,), jnp.int32)])
    target = jnp.where(
        jnp.arange(target.shape[0]) == tile_count[0], blocks - 1, target
    ).astype(jnp.int32)
    source = jnp.where(
        jnp.arange(source.shape[0]) == tile_count[0], edge_source, source
    ).astype(jnp.int32)
    live = tile_count + has_next
    first = (me * blocks).astype(jnp.int32).reshape(1)
    acc, dense = tiles(live, target, source, factor, first, everyone, jnp.stack([near, state]))
    returned = lax.psum_scatter(dense, AXES, scatter_dimension=0, tiled=True)
    out = (acc + returned).transpose(1, 0, 2).reshape(ROWS, blocks * width)
    return out[:3], out[4:7]


def solution(mesh):
    placed = (
        P(None, AXES),
        P(None, AXES),
        P(AXES),
        P(),
        P(AXES, None),
        P(AXES),
        P(AXES),
        P(AXES),
    )
    return jax.shard_map(
        local,
        mesh=mesh,
        in_specs=placed,
        out_specs=(P(None, AXES), P(None, AXES)),
        check_vma=False,
    )
```

```python
import functools
import math

import jax
import jax.numpy as jnp
from jax import lax
from jax.experimental import pallas as pl
from jax.experimental.pallas import tpu as pltpu
from jax.sharding import PartitionSpec as P

AXES = ("rotor", "blk")
green_scale = 1.0 / (4.0 * math.pi)
smooth_scale = 2.0 * math.e
log2_e = math.log2(math.e)
ROWS = 8
f32, bf16 = jnp.float32, jnp.bfloat16


def split3(v):
    hi = v.astype(bf16)
    rest = v - hi.astype(f32)
    mid = rest.astype(bf16)
    return hi, mid, (rest - mid.astype(f32)).astype(bf16)


def split2(v):
    hi = v.astype(bf16)
    return hi, (v - hi.astype(f32)).astype(bf16)


def roll(v, up):
    return pltpu.roll(v, (ROWS - up) % ROWS, 0)


def row_ids(width):
    return lax.broadcasted_iota(jnp.int32, (ROWS, width), 0)


def features(raw, factor):
    row = row_ids(raw.shape[1])
    base = jnp.where(row >= 3, raw * factor, raw)
    xx = jnp.where(row < 3, base, roll(base, 5))
    aa = jnp.where(row < 3, roll(base, 3), base)
    norm = jnp.sum(jnp.where(row < 3, base * base, 0.0), axis=0, keepdims=True)
    along = jnp.sum(jnp.where(row < 3, base * aa, 0.0), axis=0, keepdims=True)
    base = jnp.where(row == 6, norm, jnp.where(row == 7, along, base))
    x1, x2, a1, a2 = roll(xx, 1), roll(xx, 2), roll(aa, 1), roll(aa, 2)
    spin = jnp.where(row < 3, x1 * a2 - x2 * a1, 0.0)
    group = jnp.where(row < 5, aa, jnp.where(row == 5, 1.0, 0.0))
    hi, lo = split2(jnp.concatenate([group, spin], axis=0))
    values = jnp.concatenate([hi, lo], axis=0)
    return base, values, (x1, x2, a1, a2, aa)


def source_front(base):
    row = row_ids(base.shape[1])
    full = jnp.concatenate([base, jnp.where(row == 0, 1.0, 0.0)], axis=0)
    hi, mid, lo = split3(full)
    return jnp.concatenate([hi, hi, mid, mid, hi, lo], axis=0)


def target_front(base):
    row = row_ids(base.shape[1])
    norm, along = base[6:7], base[7:8]
    zero = jnp.zeros_like(base)
    dist = jnp.concatenate(
        [
            jnp.where(row < 3, -2.0 * base, jnp.where(row == 6, 1.0, 0.0)),
            jnp.where(row == 0, norm + 1.0, zero),
        ],
        axis=0,
    )
    to_target = jnp.concatenate(
        [jnp.where(row < 3, -roll(base, 3), 0.0), jnp.where(row == 0, along, zero)], axis=0
    )
    shifted = roll(base, 5)
    to_source = jnp.concatenate(
        [
            jnp.where((row >= 3) & (row < 6), -shifted, jnp.where(row == 7, 1.0, 0.0)),
            zero,
        ],
        axis=0,
    )
    hi, mid, lo = split3(jnp.concatenate([dist, to_target, to_source], axis=1))
    return jnp.concatenate([hi, mid, hi, mid, lo, hi], axis=0)


def combine(sums, own):
    width = sums.shape[1] // 3
    x1, x2, a1, a2, aa = own
    half = sums.shape[0] // 2
    sums = sums[:half] + sums[half:]
    ga, la, ea = (sums[:ROWS, i * width : (i + 1) * width] for i in range(3))
    gs, ls = (sums[ROWS:, i * width : (i + 1) * width] for i in range(2))
    ga1, ga2, la1, la2 = roll(ga, 1), roll(ga, 2), roll(la, 1), roll(la, 2)
    u = green_scale * (gs - (x1 * ga2 - x2 * ga1))
    w = (
        (3.0 * green_scale) * (x1 * la2 - x2 * la1 - ls)
        - green_scale * (a1 * ga2 - a2 * ga1)
        + smooth_scale * (ea - ea[5:6] * aa)
    )
    return jnp.where(row_ids(width) < 4, u, roll(w, 4))


def pair(front_s, values_s, own_s, front_t, values_t, own_t, both):
    width = values_s.shape[1]
    d = lax.dot_general(
        front_s, front_t, (((0,), (0,)), ((), ())), preferred_element_type=f32
    )
    p = d[:, :width]
    inv = lax.rsqrt(p)
    inv2 = inv * inv
    g = inv2 * inv
    h = g * inv2
    e = jnp.exp2(p * (-log2_e))
    g2, e2 = split2(g), split2(e)
    l2 = split2(h * d[:, width : 2 * width])
    ahead = jnp.concatenate(
        [jnp.concatenate([g2[i], l2[i], e2[i]], axis=1) for i in range(2)], axis=0
    )
    lhs = jnp.concatenate([values_s, values_s], axis=1)
    to_t = combine(jnp.dot(lhs, ahead, preferred_element_type=f32), own_t)
    if not both:
        return to_t, None
    m2 = split2(h * d[:, 2 * width :])
    back = jnp.concatenate(
        [jnp.concatenate([v[0], v[1]], axis=1) for v in (g2, m2, e2)], axis=0
    )
    lhs = jnp.concatenate([values_t, values_t], axis=1)
    sums = lax.dot_general(lhs, back, (((1,), (1,)), ((), ())), preferred_element_type=f32)
    return to_t, combine(sums, own_s)


def exchange_kernel(rows, out, landing, send, receive):
    n = rows.shape[0]
    n_blk = lax.axis_size("blk")
    me = lax.axis_index("rotor") * n_blk + lax.axis_index("blk")

    def where(peer):
        return (peer // n_blk, lax.rem(peer, n_blk))

    barrier = pltpu.get_barrier_semaphore()

    def greet(d, carry):
        pl.semaphore_signal(
            barrier,
            inc=1,
            device_id=where(lax.rem(me + d, n)),
            device_id_type=pl.DeviceIdType.MESH,
        )
        return carry

    lax.fori_loop(1, n, greet, 0)
    pl.semaphore_wait(barrier, n - 1)

    def copy(d):
        peer = lax.rem(me + d, n)
        return pltpu.make_async_remote_copy(
            src_ref=rows.at[peer],
            dst_ref=landing.at[me],
            send_sem=send.at[d],
            recv_sem=receive.at[d],
            device_id=where(peer),
            device_id_type=pl.DeviceIdType.MESH,
        )

    def start(d, carry):
        copy(d).start()
        return carry

    lax.fori_loop(1, n, start, 0)
    landing[me] = rows[me]

    def finish(d, carry):
        copy(d).wait()
        return carry

    lax.fori_loop(1, n, finish, 0)
    out[...] = landing[...]


def gather_kernel(asked, state, out):
    def step(p, carry):
        block = state[jnp.maximum(asked[p], 0)]
        out[pl.ds(p * 6, 6)] = block[:6]
        return carry

    lax.fori_loop(0, asked.shape[0], step, 0)


def prepare(state, factor_of, front, values, own, sources=None):
    def step(k, carry):
        base, vals, perm = features(state[k], factor_of(k))
        front[k] = target_front(base)
        values[k] = vals
        for i, v in enumerate(perm):
            own[k, i] = v
        if sources is not None:
            sources[k] = source_front(base)
        return carry

    lax.fori_loop(0, state.shape[0], step, 0)


def near_kernel(factor, ends, state, out, total, front, values, own, sources):
    prepare(state, lambda k: factor[k], front, values, own, sources)
    blocks = out.shape[0]

    def held(k):
        return values[k], tuple(own[k, i] for i in range(5))

    def chain(k):
        vs, os = held(k + 1)
        vt, ot = held(k)
        return pair(sources[k + 1], vs, os, front[k], vt, ot, True)

    def alone(k):
        v, o = held(k)
        return pair(sources[k], v, o, front[k], v, o, False)[0]

    total[1] = chain(0)[1] * ends[0]

    def both(k, carry):
        itself = alone(k)
        to_t, to_s = chain(k)
        total[k] += itself + to_t
        total[k + 1] = to_s
        return carry

    lax.fori_loop(1, blocks, both, 0)
    total[blocks] += alone(blocks) + chain(blocks)[0] * ends[1]
    out[...] = total[1 : blocks + 1]


def tile_kernel(
    part, live, target, place, share, origin, factor, first, state, arrived, before, acc, back,
    front, values, own, chosen,
):
    mine = acc.shape[0]
    prepare(state, lambda k: factor[first[0] + k], front, values, own)
    acc[...] = before[...]

    def choose(c, held):
        chosen[held] = c
        return held + (share[c] == part).astype(jnp.int32)

    count = lax.fori_loop(0, live[0], choose, jnp.int32(0))
    width = acc.shape[2]

    def one(i):
        c = chosen[i]
        t, p = target[c], place[c]
        raw = arrived[pl.ds(p * 6, 6)]
        raw = jnp.concatenate([raw, jnp.zeros((2, width), f32)], axis=0)
        base, vs, os = features(raw, factor[origin[c]])
        vt, ot = values[t], tuple(own[t, i] for i in range(5))
        return t, p, pair(source_front(base), vs, os, front[t], vt, ot, True)

    def add(t, p, terms):
        acc[t] += terms[0]
        back[pl.ds(p * 6, 6)] = jnp.concatenate([terms[1][:3], terms[1][4:7]], axis=0)

    def step(i, carry):
        add(*one(i))
        return carry

    def two(i, carry):
        first_one, second_one = one(2 * i), one(2 * i + 1)
        add(*first_one)
        add(*second_one)
        return carry

    lax.fori_loop(0, count // 2, two, 0)
    lax.fori_loop(count // 2 * 2, count, step, 0)


def final_kernel(*refs):
    asked, near, acc = refs[:3]
    returned, (velocity, rate, total) = refs[3:-3], refs[-3:]
    blocks, _, width = near.shape
    total[pl.ds(0, blocks)] = near[...] + acc[...]
    slots = asked.shape[0] // len(returned)
    for i, got in enumerate(returned):

        def step(p, carry):
            index = asked[i * slots + p]
            index = jnp.where(index < 0, blocks, index)
            terms = got[pl.ds(p * 6, 6)]
            gap = jnp.zeros((1, width), f32)
            total[index] += jnp.concatenate([terms[:3], gap, terms[3:], gap], axis=0)
            return carry

        lax.fori_loop(0, slots, step, 0)
    for k in range(blocks):
        velocity[:, k * width : (k + 1) * width] = total[k][:3]
        rate[:, k * width : (k + 1) * width] = total[k][4:7]


def scratch(blocks, width):
    return [
        pltpu.VMEM((blocks, 96, 3 * width), bf16),
        pltpu.VMEM((blocks, 32, width), bf16),
        pltpu.VMEM((blocks, 5, ROWS, width), f32),
    ]


smem = pl.BlockSpec(memory_space=pltpu.SMEM)
vmem = pl.BlockSpec(memory_space=pltpu.VMEM)
params = pltpu.CompilerParams(vmem_limit_bytes=24 * 2**20)


def exchange(rows):
    n = rows.shape[0]
    return pl.pallas_call(
        exchange_kernel,
        out_shape=jax.ShapeDtypeStruct(rows.shape, f32),
        in_specs=[vmem],
        out_specs=vmem,
        scratch_shapes=[
            pltpu.VMEM(rows.shape, f32),
            pltpu.SemaphoreType.DMA((n,)),
            pltpu.SemaphoreType.DMA((n,)),
        ],
        compiler_params=pltpu.CompilerParams(collective_id=0, has_side_effects=True),
    )(rows)


def gather(asked, state):
    return pl.pallas_call(
        gather_kernel,
        out_shape=jax.ShapeDtypeStruct((asked.shape[0] * 6, state.shape[2]), f32),
        in_specs=[smem, vmem],
        out_specs=vmem,
        compiler_params=params,
    )(asked, state)


def near_field(factor, ends, state):
    padded, _, width = state.shape
    return pl.pallas_call(
        near_kernel,
        out_shape=jax.ShapeDtypeStruct((padded - 2, ROWS, width), f32),
        in_specs=[smem, smem, vmem],
        out_specs=vmem,
        scratch_shapes=[pltpu.VMEM((padded, ROWS, width), f32)]
        + scratch(padded, width)
        + [pltpu.VMEM((padded, 96, width), bf16)],
        compiler_params=params,
        cost_estimate=pl.CostEstimate(
            flops=20 * 10**9, bytes_accessed=2**20, transcendentals=0
        ),
    )(factor, ends, state)


def tiles(part, scalars, state, arrived, before):
    blocks, _, width = state.shape
    return pl.pallas_call(
        functools.partial(tile_kernel, part),
        out_shape=(
            jax.ShapeDtypeStruct(state.shape, f32),
            jax.ShapeDtypeStruct(arrived.shape, f32),
        ),
        in_specs=[smem] * len(scalars) + [vmem] * 3,
        out_specs=(vmem, vmem),
        scratch_shapes=scratch(blocks, width)
        + [pltpu.SMEM((scalars[1].shape[0] + 1,), jnp.int32)],
        compiler_params=params,
        cost_estimate=pl.CostEstimate(
            flops=30 * 10**9, bytes_accessed=2**20, transcendentals=0
        ),
    )(*scalars, state, arrived, before)


def finish(asked, near, acc, returned):
    blocks, _, width = near.shape
    shape = jax.ShapeDtypeStruct((3, blocks * width), f32)
    return pl.pallas_call(
        final_kernel,
        out_shape=(shape, shape),
        in_specs=[smem] + [vmem] * (2 + len(returned)),
        out_specs=(vmem, vmem),
        scratch_shapes=[pltpu.VMEM((blocks + 1, ROWS, width), f32)],
        compiler_params=params,
    )(asked, near, acc, *returned)


PARTS = 2


def local(
    positions,
    strengths,
    blade_of_block,
    circulation,
    tile_source_dev,
    tile_source_blk,
    tile_target,
    tile_count,
):
    blocks = blade_of_block.shape[0]
    width = positions.shape[1] // blocks
    n_blk = lax.axis_size("blk")
    devices = lax.axis_size("rotor") * n_blk
    place = lax.axis_index("blk")
    me = lax.axis_index("rotor") * n_blk + place
    capacity = tile_target.shape[0]
    slot_count = max(2, (3 * capacity + 2 * devices - 1) // (2 * devices))
    each = -(-slot_count // PARTS)

    source_dev = tile_source_dev[:, 0]
    ids = jnp.arange(capacity, dtype=jnp.int32)
    earlier = (source_dev[:, None] == source_dev[None, :]) & (ids[:, None] > ids[None, :])
    rank = jnp.sum(earlier.astype(jnp.int32), axis=1)
    share = rank // each
    spot = source_dev * each + rank % each
    origin = source_dev * blocks + tile_source_blk
    ask = jnp.where(ids < tile_count[0], tile_source_blk, -1)
    peer_hot = source_dev[None, :] == jnp.arange(devices, dtype=jnp.int32)[:, None]
    rank_hot = rank[None, :] == jnp.arange(PARTS * each, dtype=jnp.int32)[:, None]
    request = (
        jnp.sum(
            jnp.where(
                peer_hot[:, None, :] & rank_hot[None, :, :], (ask + 1)[None, None, :], 0
            ),
            axis=2,
        )
        - 1
    )

    magnitude = jnp.sqrt(jnp.sum(strengths * strengths, axis=0)).reshape(blocks, width).sum(axis=1)
    facts = jnp.concatenate([magnitude, blade_of_block.astype(f32)])
    rows = jnp.concatenate(
        [
            request.astype(f32),
            jnp.broadcast_to(facts[None, :], (devices, 2 * blocks)),
        ],
        axis=1,
    )
    used = PARTS * each
    rows = jnp.pad(rows, ((0, 0), (0, -rows.shape[1] % 128)))
    got = exchange(rows[:, None, :])[:, 0]
    asked = got[:, :used].astype(jnp.int32)
    asked = asked.reshape(devices, PARTS, each).transpose(1, 0, 2)
    member = (
        got[:, used + blocks : used + 2 * blocks].reshape(-1, 1)
        == jnp.arange(circulation.shape[0], dtype=jnp.int32).astype(f32)[None, :]
    ).astype(f32)
    totals = jnp.sum(member * got[:, used : used + blocks].reshape(-1, 1), axis=0)
    counted = jnp.sum(member, axis=0) * width
    blade_factor = circulation / (totals / jnp.maximum(counted, 1.0) + 1e-06)
    factor = jnp.sum(member * blade_factor[None, :], axis=1)

    state = jnp.concatenate(
        [positions, strengths, jnp.zeros((2, positions.shape[1]), f32)], axis=0
    )
    state = state.reshape(ROWS, blocks, width).transpose(1, 0, 2)

    def swap(flat):
        return lax.all_to_all(flat, AXES, split_axis=0, concat_axis=0, tiled=True)

    up = [(i, i + 1) for i in range(n_blk - 1)]
    down = [(i + 1, i) for i in range(n_blk - 1)]
    padded = jnp.concatenate(
        [
            lax.ppermute(state[blocks - 1 :], "blk", up),
            state,
            lax.ppermute(state[:1], "blk", down),
        ],
        axis=0,
    )
    state, padded = lax.optimization_barrier((state, padded))
    arrived = [swap(gather(asked[i].reshape(-1), state)) for i in range(PARTS)]
    ends = jnp.stack([place > 0, place < n_blk - 1]).astype(f32)
    around = jnp.concatenate([jnp.zeros((1,), f32), factor, jnp.zeros((1,), f32)])
    near_factor = lax.dynamic_slice_in_dim(around, me * blocks, blocks + 2)
    first = (me * blocks).astype(jnp.int32).reshape(1)
    scalars = (tile_count, tile_target, spot, share, origin, factor, first)
    acc = jnp.zeros((blocks, ROWS, width), f32)
    returned = []
    for i in range(PARTS):
        acc, back = tiles(i, scalars, state, arrived[i], acc)
        returned.append(swap(back))
    padded, acc = lax.optimization_barrier((padded, acc))
    near = near_field(near_factor, ends, padded)
    return finish(asked.reshape(-1), near, acc, returned)


def solution(mesh):
    placed = (
        P(None, AXES),
        P(None, AXES),
        P(AXES),
        P(),
        P(AXES, None),
        P(AXES),
        P(AXES),
        P(AXES),
    )
    return jax.shard_map(
        local,
        mesh=mesh,
        in_specs=placed,
        out_specs=(P(None, AXES), P(None, AXES)),
        check_vma=False,
    )
```

```python
import functools
import math

import jax
import jax.numpy as jnp
from jax import lax
from jax.experimental import pallas as pl
from jax.experimental.pallas import tpu as pltpu
from jax.sharding import PartitionSpec as P

AXES = ("rotor", "blk")
green_scale = 1.0 / (4.0 * math.pi)
smooth_scale = 2.0 * math.e
log2_e = math.log2(math.e)
ROWS = 8
f32, bf16 = jnp.float32, jnp.bfloat16


def split3(v):
    hi = v.astype(bf16)
    rest = v - hi.astype(f32)
    mid = rest.astype(bf16)
    return hi, mid, (rest - mid.astype(f32)).astype(bf16)


def split2(v):
    hi = v.astype(bf16)
    return hi, (v - hi.astype(f32)).astype(bf16)


def roll(v, up):
    return pltpu.roll(v, (ROWS - up) % ROWS, 0)


def row_ids(width):
    return lax.broadcasted_iota(jnp.int32, (ROWS, width), 0)


def features(raw, factor):
    row = row_ids(raw.shape[1])
    base = jnp.where(row >= 3, raw * factor, raw)
    xx = jnp.where(row < 3, base, roll(base, 5))
    aa = jnp.where(row < 3, roll(base, 3), base)
    norm = jnp.sum(jnp.where(row < 3, base * base, 0.0), axis=0, keepdims=True)
    along = jnp.sum(jnp.where(row < 3, base * aa, 0.0), axis=0, keepdims=True)
    base = jnp.where(row == 6, norm, jnp.where(row == 7, along, base))
    x1, x2, a1, a2 = roll(xx, 1), roll(xx, 2), roll(aa, 1), roll(aa, 2)
    spin = jnp.where(row < 3, x1 * a2 - x2 * a1, 0.0)
    group = jnp.where(row < 5, aa, jnp.where(row == 5, 1.0, 0.0))
    hi, lo = split2(jnp.concatenate([group, spin], axis=0))
    values = jnp.concatenate([hi, lo], axis=0)
    return base, values, (x1, x2, a1, a2, aa)


def source_front(base):
    row = row_ids(base.shape[1])
    full = jnp.concatenate([base, jnp.where(row == 0, 1.0, 0.0)], axis=0)
    hi, mid, lo = split3(full)
    return jnp.concatenate([hi, hi, mid, mid, hi, lo], axis=0)


def target_front(base):
    row = row_ids(base.shape[1])
    norm, along = base[6:7], base[7:8]
    zero = jnp.zeros_like(base)
    dist = jnp.concatenate(
        [
            jnp.where(row < 3, -2.0 * base, jnp.where(row == 6, 1.0, 0.0)),
            jnp.where(row == 0, norm + 1.0, zero),
        ],
        axis=0,
    )
    to_target = jnp.concatenate(
        [jnp.where(row < 3, -roll(base, 3), 0.0), jnp.where(row == 0, along, zero)], axis=0
    )
    shifted = roll(base, 5)
    to_source = jnp.concatenate(
        [
            jnp.where((row >= 3) & (row < 6), -shifted, jnp.where(row == 7, 1.0, 0.0)),
            zero,
        ],
        axis=0,
    )
    hi, mid, lo = split3(jnp.concatenate([dist, to_target, to_source], axis=1))
    return jnp.concatenate([hi, mid, hi, mid, lo, hi], axis=0)


def combine(sums, own):
    width = sums.shape[1] // 3
    x1, x2, a1, a2, aa = own
    half = sums.shape[0] // 2
    sums = sums[:half] + sums[half:]
    ga, la, ea = (sums[:ROWS, i * width : (i + 1) * width] for i in range(3))
    gs, ls = (sums[ROWS:, i * width : (i + 1) * width] for i in range(2))
    ga1, ga2, la1, la2 = roll(ga, 1), roll(ga, 2), roll(la, 1), roll(la, 2)
    u = green_scale * (gs - (x1 * ga2 - x2 * ga1))
    w = (
        (3.0 * green_scale) * (x1 * la2 - x2 * la1 - ls)
        - green_scale * (a1 * ga2 - a2 * ga1)
        + smooth_scale * (ea - ea[5:6] * aa)
    )
    return jnp.where(row_ids(width) < 4, u, roll(w, 4))


def pair(front_s, values_s, own_s, front_t, values_t, own_t, both):
    width = values_s.shape[1]
    d = lax.dot_general(
        front_s, front_t, (((0,), (0,)), ((), ())), preferred_element_type=f32
    )
    p = d[:, :width]
    inv = lax.rsqrt(p)
    inv2 = inv * inv
    g = inv2 * inv
    h = g * inv2
    e = jnp.exp2(p * (-log2_e))
    g2, e2 = split2(g), split2(e)
    l2 = split2(h * d[:, width : 2 * width])
    ahead = jnp.concatenate(
        [jnp.concatenate([g2[i], l2[i], e2[i]], axis=1) for i in range(2)], axis=0
    )
    lhs = jnp.concatenate([values_s, values_s], axis=1)
    to_t = combine(jnp.dot(lhs, ahead, preferred_element_type=f32), own_t)
    if not both:
        return to_t, None
    m2 = split2(h * d[:, 2 * width :])
    back = jnp.concatenate(
        [jnp.concatenate([v[0], v[1]], axis=1) for v in (g2, m2, e2)], axis=0
    )
    lhs = jnp.concatenate([values_t, values_t], axis=1)
    sums = lax.dot_general(lhs, back, (((1,), (1,)), ((), ())), preferred_element_type=f32)
    return to_t, combine(sums, own_s)


def exchange_kernel(rows, state, out, edges, landing, sides, send, receive, side_send, side_get):
    n = rows.shape[0]
    n_blk = lax.axis_size("blk")
    rotor, place = lax.axis_index("rotor"), lax.axis_index("blk")
    me = rotor * n_blk + place

    def where(peer):
        return (peer // n_blk, lax.rem(peer, n_blk))

    barrier = pltpu.get_barrier_semaphore()

    def greet(d, carry):
        pl.semaphore_signal(
            barrier,
            inc=1,
            device_id=where(lax.rem(me + d, n)),
            device_id_type=pl.DeviceIdType.MESH,
        )
        return carry

    lax.fori_loop(1, n, greet, 0)
    pl.semaphore_wait(barrier, n - 1)

    def copy(d):
        peer = lax.rem(me + d, n)
        return pltpu.make_async_remote_copy(
            src_ref=rows.at[peer],
            dst_ref=landing.at[me],
            send_sem=send.at[d],
            recv_sem=receive.at[d],
            device_id=where(peer),
            device_id_type=pl.DeviceIdType.MESH,
        )

    def side(i):
        block, step = ((state.shape[0] - 1, 1), (0, n_blk - 1))[i]
        return pltpu.make_async_remote_copy(
            src_ref=state.at[block],
            dst_ref=sides.at[i],
            send_sem=side_send.at[i],
            recv_sem=side_get.at[i],
            device_id=(rotor, lax.rem(place + step, n_blk)),
            device_id_type=pl.DeviceIdType.MESH,
        )

    def start(d, carry):
        copy(d).start()
        return carry

    lax.fori_loop(1, n, start, 0)
    side(0).start()
    side(1).start()
    landing[me] = rows[me]

    def finish(d, carry):
        copy(d).wait()
        return carry

    lax.fori_loop(1, n, finish, 0)
    side(0).wait()
    side(1).wait()
    out[...] = landing[...]
    edges[...] = sides[...]


def gather_kernel(asked, state, out):
    def step(p, carry):
        block = state[jnp.maximum(asked[p], 0)]
        out[pl.ds(p * 6, 6)] = block[:6]
        return carry

    lax.fori_loop(0, asked.shape[0], step, 0)


def prepare(state, factor_of, front, values, own, sources=None):
    def step(k, carry):
        base, vals, perm = features(state[k], factor_of(k))
        front[k] = target_front(base)
        values[k] = vals
        for i, v in enumerate(perm):
            own[k, i] = v
        if sources is not None:
            sources[k] = source_front(base)
        return carry

    lax.fori_loop(0, state.shape[0], step, 0)


def near_kernel(factor, ends, state, out, total, front, values, own, sources):
    prepare(state, lambda k: factor[k], front, values, own, sources)
    blocks = out.shape[0]

    def held(k):
        return values[k], tuple(own[k, i] for i in range(5))

    def chain(k):
        vs, os = held(k + 1)
        vt, ot = held(k)
        return pair(sources[k + 1], vs, os, front[k], vt, ot, True)

    def alone(k):
        v, o = held(k)
        return pair(sources[k], v, o, front[k], v, o, False)[0]

    total[...] = jnp.zeros_like(total)
    group = math.gcd(blocks, 4)

    def several(j, carry):
        ks = [j * group + i + 1 for i in range(group)]
        terms = [(alone(k), chain(k - 1)) for k in ks]
        for k, (itself, (to_t, to_s)) in zip(ks, terms):
            total[k - 1] += to_t * jnp.where(k == 1, 0.0, 1.0)
            total[k] += itself + to_s * jnp.where(k == 1, ends[0], 1.0)
        return carry

    lax.fori_loop(0, blocks // group, several, 0)
    total[blocks] += chain(blocks)[0] * ends[1]
    out[...] = total[1 : blocks + 1]


def tile_kernel(
    part, live, target, place, share, origin, factor, first, state, arrived, before, acc, back,
    front, values, own, chosen,
):
    mine = acc.shape[0]
    prepare(state, lambda k: factor[first[0] + k], front, values, own)
    acc[...] = before[...]

    def choose(c, held):
        chosen[held] = c
        return held + (share[c] == part).astype(jnp.int32)

    count = lax.fori_loop(0, live[0], choose, jnp.int32(0))
    width = acc.shape[2]

    def one(i):
        c = chosen[i]
        t, p = target[c], place[c]
        raw = arrived[pl.ds(p * 6, 6)]
        raw = jnp.concatenate([raw, jnp.zeros((2, width), f32)], axis=0)
        base, vs, os = features(raw, factor[origin[c]])
        vt, ot = values[t], tuple(own[t, i] for i in range(5))
        return t, p, pair(source_front(base), vs, os, front[t], vt, ot, True)

    def step(j, carry):
        at = [j * GROUP + i for i in range(GROUP)]
        done = [one(jnp.minimum(i, count - 1)) for i in at]
        for i, (t, p, (to_t, to_s)) in zip(at, done):
            acc[t] += to_t * jnp.where(i < count, 1.0, 0.0)
            back[pl.ds(p * 6, 6)] = jnp.concatenate([to_s[:3], to_s[4:7]], axis=0)
        return carry

    lax.fori_loop(0, (count + GROUP - 1) // GROUP, step, 0)


def final_kernel(*refs):
    asked, near, acc = refs[:3]
    returned, (velocity, rate, total) = refs[3:-3], refs[-3:]
    blocks, _, width = near.shape
    total[pl.ds(0, blocks)] = near[...] + acc[...]
    slots = asked.shape[0] // len(returned)
    for i, got in enumerate(returned):

        def step(p, carry):
            index = asked[i * slots + p]
            index = jnp.where(index < 0, blocks, index)
            terms = got[pl.ds(p * 6, 6)]
            gap = jnp.zeros((1, width), f32)
            total[index] += jnp.concatenate([terms[:3], gap, terms[3:], gap], axis=0)
            return carry

        lax.fori_loop(0, slots, step, 0)
    for k in range(blocks):
        velocity[:, k * width : (k + 1) * width] = total[k][:3]
        rate[:, k * width : (k + 1) * width] = total[k][4:7]


def scratch(blocks, width):
    return [
        pltpu.VMEM((blocks, 96, 3 * width), bf16),
        pltpu.VMEM((blocks, 32, width), bf16),
        pltpu.VMEM((blocks, 5, ROWS, width), f32),
    ]


smem = pl.BlockSpec(memory_space=pltpu.SMEM)
vmem = pl.BlockSpec(memory_space=pltpu.VMEM)
params = pltpu.CompilerParams(vmem_limit_bytes=24 * 2**20)


def exchange(rows, state):
    n = rows.shape[0]
    edges = jax.ShapeDtypeStruct((2,) + state.shape[1:], f32)
    return pl.pallas_call(
        exchange_kernel,
        out_shape=(jax.ShapeDtypeStruct(rows.shape, f32), edges),
        in_specs=[vmem, vmem],
        out_specs=(vmem, vmem),
        scratch_shapes=[
            pltpu.VMEM(rows.shape, f32),
            pltpu.VMEM(edges.shape, f32),
            pltpu.SemaphoreType.DMA((n,)),
            pltpu.SemaphoreType.DMA((n,)),
            pltpu.SemaphoreType.DMA((2,)),
            pltpu.SemaphoreType.DMA((2,)),
        ],
        compiler_params=pltpu.CompilerParams(collective_id=0, has_side_effects=True),
    )(rows, state)


def gather(asked, state):
    return pl.pallas_call(
        gather_kernel,
        out_shape=jax.ShapeDtypeStruct((asked.shape[0] * 6, state.shape[2]), f32),
        in_specs=[smem, vmem],
        out_specs=vmem,
        compiler_params=params,
    )(asked, state)


def near_field(factor, ends, state):
    padded, _, width = state.shape
    return pl.pallas_call(
        near_kernel,
        out_shape=jax.ShapeDtypeStruct((padded - 2, ROWS, width), f32),
        in_specs=[smem, smem, vmem],
        out_specs=vmem,
        scratch_shapes=[pltpu.VMEM((padded, ROWS, width), f32)]
        + scratch(padded, width)
        + [pltpu.VMEM((padded, 96, width), bf16)],
        compiler_params=params,
        cost_estimate=pl.CostEstimate(
            flops=20 * 10**9, bytes_accessed=2**20, transcendentals=0
        ),
    )(factor, ends, state)


def tiles(part, scalars, state, arrived, before):
    blocks, _, width = state.shape
    return pl.pallas_call(
        functools.partial(tile_kernel, part),
        out_shape=(
            jax.ShapeDtypeStruct(state.shape, f32),
            jax.ShapeDtypeStruct(arrived.shape, f32),
        ),
        in_specs=[smem] * len(scalars) + [vmem] * 3,
        out_specs=(vmem, vmem),
        scratch_shapes=scratch(blocks, width)
        + [pltpu.SMEM((scalars[1].shape[0] + 1,), jnp.int32)],
        compiler_params=params,
        cost_estimate=pl.CostEstimate(
            flops=30 * 10**9, bytes_accessed=2**20, transcendentals=0
        ),
    )(*scalars, state, arrived, before)


def finish(asked, near, acc, returned):
    blocks, _, width = near.shape
    shape = jax.ShapeDtypeStruct((3, blocks * width), f32)
    return pl.pallas_call(
        final_kernel,
        out_shape=(shape, shape),
        in_specs=[smem] + [vmem] * (2 + len(returned)),
        out_specs=(vmem, vmem),
        scratch_shapes=[pltpu.VMEM((blocks + 1, ROWS, width), f32)],
        compiler_params=params,
    )(asked, near, acc, *returned)


PARTS = 2
GROUP = 8


def local(
    positions,
    strengths,
    blade_of_block,
    circulation,
    tile_source_dev,
    tile_source_blk,
    tile_target,
    tile_count,
):
    blocks = blade_of_block.shape[0]
    width = positions.shape[1] // blocks
    n_blk = lax.axis_size("blk")
    devices = lax.axis_size("rotor") * n_blk
    place = lax.axis_index("blk")
    me = lax.axis_index("rotor") * n_blk + place
    capacity = tile_target.shape[0]
    slot_count = max(2, (3 * capacity + 2 * devices - 1) // (2 * devices))
    each = -(-slot_count // PARTS)

    source_dev = tile_source_dev[:, 0]
    ids = jnp.arange(capacity, dtype=jnp.int32)
    earlier = (source_dev[:, None] == source_dev[None, :]) & (ids[:, None] > ids[None, :])
    rank = jnp.sum(earlier.astype(jnp.int32), axis=1)
    share = rank // each
    spot = source_dev * each + rank % each
    origin = source_dev * blocks + tile_source_blk
    ask = jnp.where(ids < tile_count[0], tile_source_blk, -1)
    peer_hot = source_dev[None, :] == jnp.arange(devices, dtype=jnp.int32)[:, None]
    rank_hot = rank[None, :] == jnp.arange(PARTS * each, dtype=jnp.int32)[:, None]
    request = (
        jnp.sum(
            jnp.where(
                peer_hot[:, None, :] & rank_hot[None, :, :], (ask + 1)[None, None, :], 0
            ),
            axis=2,
        )
        - 1
    )

    magnitude = jnp.sqrt(jnp.sum(strengths * strengths, axis=0)).reshape(blocks, width).sum(axis=1)
    facts = jnp.concatenate([magnitude, blade_of_block.astype(f32)])
    rows = jnp.concatenate(
        [
            request.astype(f32),
            jnp.broadcast_to(facts[None, :], (devices, 2 * blocks)),
        ],
        axis=1,
    )
    used = PARTS * each
    rows = jnp.pad(rows, ((0, 0), (0, -rows.shape[1] % 128)))
    state = jnp.concatenate(
        [positions, strengths, jnp.zeros((2, positions.shape[1]), f32)], axis=0
    )
    state = state.reshape(ROWS, blocks, width).transpose(1, 0, 2)
    got, edges = exchange(rows[:, None, :], state)
    got = got[:, 0]
    asked = got[:, :used].astype(jnp.int32)
    asked = asked.reshape(devices, PARTS, each).transpose(1, 0, 2)
    member = (
        got[:, used + blocks : used + 2 * blocks].reshape(-1, 1)
        == jnp.arange(circulation.shape[0], dtype=jnp.int32).astype(f32)[None, :]
    ).astype(f32)
    totals = jnp.sum(member * got[:, used : used + blocks].reshape(-1, 1), axis=0)
    counted = jnp.sum(member, axis=0) * width
    blade_factor = circulation / (totals / jnp.maximum(counted, 1.0) + 1e-06)
    factor = jnp.sum(member * blade_factor[None, :], axis=1)

    def swap(flat):
        return lax.all_to_all(flat, AXES, split_axis=0, concat_axis=0, tiled=True)

    padded = jnp.concatenate([edges[:1], state, edges[1:]], axis=0)
    arrived = [swap(gather(asked[i].reshape(-1), state)) for i in range(PARTS)]
    ends = jnp.stack([place > 0, place < n_blk - 1]).astype(f32)
    around = jnp.concatenate([jnp.zeros((1,), f32), factor, jnp.zeros((1,), f32)])
    near_factor = lax.dynamic_slice_in_dim(around, me * blocks, blocks + 2)
    first = (me * blocks).astype(jnp.int32).reshape(1)
    scalars = (tile_count, tile_target, spot, share, origin, factor, first)
    acc = jnp.zeros((blocks, ROWS, width), f32)
    returned = []
    for i in range(PARTS):
        acc, back = tiles(i, scalars, state, arrived[i], acc)
        if returned:
            back, returned[-1] = lax.optimization_barrier((back, returned[-1]))
        returned.append(swap(back))
    padded, acc = lax.optimization_barrier((padded, acc))
    near = near_field(near_factor, ends, padded)
    return finish(asked.reshape(-1), near, acc, returned)


def solution(mesh):
    placed = (
        P(None, AXES),
        P(None, AXES),
        P(AXES),
        P(),
        P(AXES, None),
        P(AXES),
        P(AXES),
        P(AXES),
    )
    return jax.shard_map(
        local,
        mesh=mesh,
        in_specs=placed,
        out_specs=(P(None, AXES), P(None, AXES)),
        check_vma=False,
    )
```

```python
import functools
import math

import jax
import jax.numpy as jnp
from jax import lax
from jax.experimental import pallas as pl
from jax.experimental.pallas import tpu as pltpu
from jax.sharding import PartitionSpec as P

AXES = ("rotor", "blk")
green_scale = 1.0 / (4.0 * math.pi)
smooth_scale = 2.0 * math.e
log2_e = math.log2(math.e)
ROWS = 8
f32, bf16 = jnp.float32, jnp.bfloat16


def split3(v):
    hi = v.astype(bf16)
    rest = v - hi.astype(f32)
    mid = rest.astype(bf16)
    return hi, mid, (rest - mid.astype(f32)).astype(bf16)


def split2(v):
    hi = v.astype(bf16)
    return hi, (v - hi.astype(f32)).astype(bf16)


def roll(v, up):
    return pltpu.roll(v, (ROWS - up) % ROWS, 0)


def row_ids(width):
    return lax.broadcasted_iota(jnp.int32, (ROWS, width), 0)


def features(raw, factor):
    row = row_ids(raw.shape[1])
    base = jnp.where(row >= 3, raw * factor, raw)
    xx = jnp.where(row < 3, base, roll(base, 5))
    aa = jnp.where(row < 3, roll(base, 3), base)
    norm = jnp.sum(jnp.where(row < 3, base * base, 0.0), axis=0, keepdims=True)
    along = jnp.sum(jnp.where(row < 3, base * aa, 0.0), axis=0, keepdims=True)
    base = jnp.where(row == 6, norm, jnp.where(row == 7, along, base))
    x1, x2, a1, a2 = roll(xx, 1), roll(xx, 2), roll(aa, 1), roll(aa, 2)
    spin = jnp.where(row < 3, x1 * a2 - x2 * a1, 0.0)
    group = jnp.where(row < 5, aa, jnp.where(row == 5, 1.0, 0.0))
    hi, lo = split2(jnp.concatenate([group, spin], axis=0))
    values = jnp.concatenate([hi, lo], axis=0)
    return base, values, (x1, x2, a1, a2, aa)


def source_front(base):
    row = row_ids(base.shape[1])
    full = jnp.concatenate([base, jnp.where(row == 0, 1.0, 0.0)], axis=0)
    hi, mid, lo = split3(full)
    return jnp.concatenate([hi, hi, mid, mid, hi, lo], axis=0)


def target_front(base):
    row = row_ids(base.shape[1])
    norm, along = base[6:7], base[7:8]
    zero = jnp.zeros_like(base)
    dist = jnp.concatenate(
        [
            jnp.where(row < 3, -2.0 * base, jnp.where(row == 6, 1.0, 0.0)),
            jnp.where(row == 0, norm + 1.0, zero),
        ],
        axis=0,
    )
    to_target = jnp.concatenate(
        [jnp.where(row < 3, -roll(base, 3), 0.0), jnp.where(row == 0, along, zero)], axis=0
    )
    shifted = roll(base, 5)
    to_source = jnp.concatenate(
        [
            jnp.where((row >= 3) & (row < 6), -shifted, jnp.where(row == 7, 1.0, 0.0)),
            zero,
        ],
        axis=0,
    )
    hi, mid, lo = split3(jnp.concatenate([dist, to_target, to_source], axis=1))
    return jnp.concatenate([hi, mid, hi, mid, lo, hi], axis=0)


def combine(sums, own):
    width = sums.shape[1] // 3
    x1, x2, a1, a2, aa = own
    half = sums.shape[0] // 2
    sums = sums[:half] + sums[half:]
    ga, la, ea = (sums[:ROWS, i * width : (i + 1) * width] for i in range(3))
    gs, ls = (sums[ROWS:, i * width : (i + 1) * width] for i in range(2))
    ga1, ga2, la1, la2 = roll(ga, 1), roll(ga, 2), roll(la, 1), roll(la, 2)
    u = green_scale * (gs - (x1 * ga2 - x2 * ga1))
    w = (
        (3.0 * green_scale) * (x1 * la2 - x2 * la1 - ls)
        - green_scale * (a1 * ga2 - a2 * ga1)
        + smooth_scale * (ea - ea[5:6] * aa)
    )
    return jnp.where(row_ids(width) < 4, u, roll(w, 4))


def pair(front_s, values_s, own_s, front_t, values_t, own_t, both):
    width = values_s.shape[1]
    d = lax.dot_general(
        front_s, front_t, (((0,), (0,)), ((), ())), preferred_element_type=f32
    )
    p = d[:, :width]
    inv = lax.rsqrt(p)
    inv2 = inv * inv
    g = inv2 * inv
    h = g * inv2
    e = jnp.exp2(p * (-log2_e))
    g2, e2 = split2(g), split2(e)
    l2 = split2(h * d[:, width : 2 * width])
    ahead = jnp.concatenate(
        [jnp.concatenate([g2[i], l2[i], e2[i]], axis=1) for i in range(2)], axis=0
    )
    lhs = jnp.concatenate([values_s, values_s], axis=1)
    to_t = combine(jnp.dot(lhs, ahead, preferred_element_type=f32), own_t)
    if not both:
        return to_t, None
    m2 = split2(h * d[:, 2 * width :])
    back = jnp.concatenate(
        [jnp.concatenate([v[0], v[1]], axis=1) for v in (g2, m2, e2)], axis=0
    )
    lhs = jnp.concatenate([values_t, values_t], axis=1)
    sums = lax.dot_general(lhs, back, (((1,), (1,)), ((), ())), preferred_element_type=f32)
    return to_t, combine(sums, own_s)


def exchange_kernel(rows, state, out, edges, landing, sides, send, receive, side_send, side_get):
    n = rows.shape[0]
    n_blk = lax.axis_size("blk")
    rotor, place = lax.axis_index("rotor"), lax.axis_index("blk")
    me = rotor * n_blk + place

    def where(peer):
        return (peer // n_blk, lax.rem(peer, n_blk))

    barrier = pltpu.get_barrier_semaphore()

    def greet(d, carry):
        pl.semaphore_signal(
            barrier,
            inc=1,
            device_id=where(lax.rem(me + d, n)),
            device_id_type=pl.DeviceIdType.MESH,
        )
        return carry

    lax.fori_loop(1, n, greet, 0)
    pl.semaphore_wait(barrier, n - 1)

    def copy(d):
        peer = lax.rem(me + d, n)
        return pltpu.make_async_remote_copy(
            src_ref=rows.at[peer],
            dst_ref=landing.at[me],
            send_sem=send.at[d],
            recv_sem=receive.at[d],
            device_id=where(peer),
            device_id_type=pl.DeviceIdType.MESH,
        )

    def side(i):
        block, step = ((state.shape[0] - 1, 1), (0, n_blk - 1))[i]
        return pltpu.make_async_remote_copy(
            src_ref=state.at[block],
            dst_ref=sides.at[i],
            send_sem=side_send.at[i],
            recv_sem=side_get.at[i],
            device_id=(rotor, lax.rem(place + step, n_blk)),
            device_id_type=pl.DeviceIdType.MESH,
        )

    def start(d, carry):
        copy(d).start()
        return carry

    lax.fori_loop(1, n, start, 0)
    side(0).start()
    side(1).start()
    landing[me] = rows[me]

    def finish(d, carry):
        copy(d).wait()
        return carry

    lax.fori_loop(1, n, finish, 0)
    side(0).wait()
    side(1).wait()
    out[...] = landing[...]
    edges[...] = sides[...]


def gather_kernel(asked, state, out):
    def step(p, carry):
        block = state[jnp.maximum(asked[p], 0)]
        out[pl.ds(p * 6, 6)] = block[:6]
        return carry

    lax.fori_loop(0, asked.shape[0], step, 0)


def prepare(state, factor_of, front, values, own, sources=None):
    def step(k, carry):
        base, vals, perm = features(state[k], factor_of(k))
        front[k] = target_front(base)
        values[k] = vals
        for i, v in enumerate(perm):
            own[k, i] = v
        if sources is not None:
            sources[k] = source_front(base)
        return carry

    lax.fori_loop(0, state.shape[0], step, 0)


def near_kernel(factor, ends, state, out, total, front, values, own, sources):
    prepare(state, lambda k: factor[k], front, values, own, sources)
    blocks = out.shape[0]

    def held(k):
        return values[k], tuple(own[k, i] for i in range(5))

    def chain(k):
        vs, os = held(k + 1)
        vt, ot = held(k)
        return pair(sources[k + 1], vs, os, front[k], vt, ot, True)

    def alone(k):
        v, o = held(k)
        return pair(sources[k], v, o, front[k], v, o, False)[0]

    total[...] = jnp.zeros_like(total)
    group = math.gcd(blocks, 4)

    def several(j, carry):
        ks = [j * group + i + 1 for i in range(group)]
        terms = [(alone(k), chain(k - 1)) for k in ks]
        for k, (itself, (to_t, to_s)) in zip(ks, terms):
            total[k - 1] += to_t * jnp.where(k == 1, 0.0, 1.0)
            total[k] += itself + to_s * jnp.where(k == 1, ends[0], 1.0)
        return carry

    lax.fori_loop(0, blocks // group, several, 0)
    total[blocks] += chain(blocks)[0] * ends[1]
    out[...] = total[1 : blocks + 1]


def tile_kernel(
    part, live, target, place, share, origin, factor, first, state, arrived, before, acc, back,
    front, values, own, chosen,
):
    mine = acc.shape[0]
    prepare(state, lambda k: factor[first[0] + k], front, values, own)
    acc[...] = before[...]

    def choose(c, held):
        chosen[held] = c
        return held + (share[c] == part).astype(jnp.int32)

    count = lax.fori_loop(0, live[0], choose, jnp.int32(0))
    width = acc.shape[2]

    def one(i):
        c = chosen[i]
        t, p = target[c], place[c]
        raw = arrived[pl.ds(p * 6, 6)]
        raw = jnp.concatenate([raw, jnp.zeros((2, width), f32)], axis=0)
        base, vs, os = features(raw, factor[origin[c]])
        vt, ot = values[t], tuple(own[t, i] for i in range(5))
        return t, p, pair(source_front(base), vs, os, front[t], vt, ot, True)

    def step(j, carry):
        at = [j * GROUP + i for i in range(GROUP)]
        done = [one(jnp.minimum(i, count - 1)) for i in at]
        for i, (t, p, (to_t, to_s)) in zip(at, done):
            acc[t] += to_t * jnp.where(i < count, 1.0, 0.0)
            back[pl.ds(p * 6, 6)] = jnp.concatenate([to_s[:3], to_s[4:7]], axis=0)
        return carry

    lax.fori_loop(0, (count + GROUP - 1) // GROUP, step, 0)


def final_kernel(*refs):
    asked, near, acc = refs[:3]
    returned, (velocity, rate, total) = refs[3:-3], refs[-3:]
    blocks, _, width = near.shape
    total[pl.ds(0, blocks)] = near[...] + acc[...]
    base = 0
    for got in returned:
        slots = got.shape[0] // 6

        def step(p, carry, got=got, base=base):
            index = asked[base + p]
            index = jnp.where(index < 0, blocks, index)
            terms = got[pl.ds(p * 6, 6)]
            gap = jnp.zeros((1, width), f32)
            total[index] += jnp.concatenate([terms[:3], gap, terms[3:], gap], axis=0)
            return carry

        lax.fori_loop(0, slots, step, 0)
        base += slots
    for k in range(blocks):
        velocity[:, k * width : (k + 1) * width] = total[k][:3]
        rate[:, k * width : (k + 1) * width] = total[k][4:7]


def scratch(blocks, width):
    return [
        pltpu.VMEM((blocks, 96, 3 * width), bf16),
        pltpu.VMEM((blocks, 32, width), bf16),
        pltpu.VMEM((blocks, 5, ROWS, width), f32),
    ]


smem = pl.BlockSpec(memory_space=pltpu.SMEM)
vmem = pl.BlockSpec(memory_space=pltpu.VMEM)
params = pltpu.CompilerParams(vmem_limit_bytes=24 * 2**20)


def exchange(rows, state):
    n = rows.shape[0]
    edges = jax.ShapeDtypeStruct((2,) + state.shape[1:], f32)
    return pl.pallas_call(
        exchange_kernel,
        out_shape=(jax.ShapeDtypeStruct(rows.shape, f32), edges),
        in_specs=[vmem, vmem],
        out_specs=(vmem, vmem),
        scratch_shapes=[
            pltpu.VMEM(rows.shape, f32),
            pltpu.VMEM(edges.shape, f32),
            pltpu.SemaphoreType.DMA((n,)),
            pltpu.SemaphoreType.DMA((n,)),
            pltpu.SemaphoreType.DMA((2,)),
            pltpu.SemaphoreType.DMA((2,)),
        ],
        compiler_params=pltpu.CompilerParams(collective_id=0, has_side_effects=True),
    )(rows, state)


def gather(asked, state):
    return pl.pallas_call(
        gather_kernel,
        out_shape=jax.ShapeDtypeStruct((asked.shape[0] * 6, state.shape[2]), f32),
        in_specs=[smem, vmem],
        out_specs=vmem,
        compiler_params=params,
    )(asked, state)


def near_field(factor, ends, state):
    padded, _, width = state.shape
    return pl.pallas_call(
        near_kernel,
        out_shape=jax.ShapeDtypeStruct((padded - 2, ROWS, width), f32),
        in_specs=[smem, smem, vmem],
        out_specs=vmem,
        scratch_shapes=[pltpu.VMEM((padded, ROWS, width), f32)]
        + scratch(padded, width)
        + [pltpu.VMEM((padded, 96, width), bf16)],
        compiler_params=params,
        cost_estimate=pl.CostEstimate(
            flops=20 * 10**9, bytes_accessed=2**20, transcendentals=0
        ),
    )(factor, ends, state)


def tiles(part, scalars, state, arrived, before):
    blocks, _, width = state.shape
    return pl.pallas_call(
        functools.partial(tile_kernel, part),
        out_shape=(
            jax.ShapeDtypeStruct(state.shape, f32),
            jax.ShapeDtypeStruct(arrived.shape, f32),
        ),
        in_specs=[smem] * len(scalars) + [vmem] * 3,
        out_specs=(vmem, vmem),
        scratch_shapes=scratch(blocks, width)
        + [pltpu.SMEM((scalars[1].shape[0] + 1,), jnp.int32)],
        compiler_params=params,
        cost_estimate=pl.CostEstimate(
            flops=30 * 10**9, bytes_accessed=2**20, transcendentals=0
        ),
    )(*scalars, state, arrived, before)


def finish(asked, near, acc, returned):
    blocks, _, width = near.shape
    shape = jax.ShapeDtypeStruct((3, blocks * width), f32)
    return pl.pallas_call(
        final_kernel,
        out_shape=(shape, shape),
        in_specs=[smem] + [vmem] * (2 + len(returned)),
        out_specs=(vmem, vmem),
        scratch_shapes=[pltpu.VMEM((blocks + 1, ROWS, width), f32)],
        compiler_params=params,
    )(asked, near, acc, *returned)


GROUP = 8


def local(
    positions,
    strengths,
    blade_of_block,
    circulation,
    tile_source_dev,
    tile_source_blk,
    tile_target,
    tile_count,
):
    blocks = blade_of_block.shape[0]
    width = positions.shape[1] // blocks
    n_blk = lax.axis_size("blk")
    devices = lax.axis_size("rotor") * n_blk
    place = lax.axis_index("blk")
    me = lax.axis_index("rotor") * n_blk + place
    capacity = tile_target.shape[0]
    slot_count = max(2, (3 * capacity + 2 * devices - 1) // (2 * devices))
    early = max(1, slot_count // 3)
    bounds = ((0, early), (early, slot_count))

    source_dev = tile_source_dev[:, 0]
    ids = jnp.arange(capacity, dtype=jnp.int32)
    earlier = (source_dev[:, None] == source_dev[None, :]) & (ids[:, None] > ids[None, :])
    rank = jnp.sum(earlier.astype(jnp.int32), axis=1)
    share = (rank >= early).astype(jnp.int32)
    spot = jnp.where(
        rank < early,
        source_dev * early + rank,
        source_dev * (slot_count - early) + rank - early,
    )
    origin = source_dev * blocks + tile_source_blk
    ask = jnp.where(ids < tile_count[0], tile_source_blk, -1)
    peer_hot = source_dev[None, :] == jnp.arange(devices, dtype=jnp.int32)[:, None]
    rank_hot = rank[None, :] == jnp.arange(slot_count, dtype=jnp.int32)[:, None]
    request = (
        jnp.sum(
            jnp.where(
                peer_hot[:, None, :] & rank_hot[None, :, :], (ask + 1)[None, None, :], 0
            ),
            axis=2,
        )
        - 1
    )

    magnitude = jnp.sqrt(jnp.sum(strengths * strengths, axis=0)).reshape(blocks, width).sum(axis=1)
    facts = jnp.concatenate([magnitude, blade_of_block.astype(f32)])
    rows = jnp.concatenate(
        [
            request.astype(f32),
            jnp.broadcast_to(facts[None, :], (devices, 2 * blocks)),
        ],
        axis=1,
    )
    used = slot_count
    rows = jnp.pad(rows, ((0, 0), (0, -rows.shape[1] % 128)))
    state = jnp.concatenate(
        [positions, strengths, jnp.zeros((2, positions.shape[1]), f32)], axis=0
    )
    state = state.reshape(ROWS, blocks, width).transpose(1, 0, 2)
    got, edges = exchange(rows[:, None, :], state)
    got = got[:, 0]
    asked = got[:, :used].astype(jnp.int32)
    asked = [asked[:, low:high].reshape(-1) for low, high in bounds]
    member = (
        got[:, used + blocks : used + 2 * blocks].reshape(-1, 1)
        == jnp.arange(circulation.shape[0], dtype=jnp.int32).astype(f32)[None, :]
    ).astype(f32)
    totals = jnp.sum(member * got[:, used : used + blocks].reshape(-1, 1), axis=0)
    counted = jnp.sum(member, axis=0) * width
    blade_factor = circulation / (totals / jnp.maximum(counted, 1.0) + 1e-06)
    factor = jnp.sum(member * blade_factor[None, :], axis=1)

    def swap(flat):
        return lax.all_to_all(flat, AXES, split_axis=0, concat_axis=0, tiled=True)

    padded = jnp.concatenate([edges[:1], state, edges[1:]], axis=0)
    arrived = [swap(gather(part, state)) for part in asked]
    ends = jnp.stack([place > 0, place < n_blk - 1]).astype(f32)
    around = jnp.concatenate([jnp.zeros((1,), f32), factor, jnp.zeros((1,), f32)])
    near_factor = lax.dynamic_slice_in_dim(around, me * blocks, blocks + 2)
    first = (me * blocks).astype(jnp.int32).reshape(1)
    scalars = (tile_count, tile_target, spot, share, origin, factor, first)
    acc = jnp.zeros((blocks, ROWS, width), f32)
    returned = []
    for i in range(len(bounds)):
        acc, back = tiles(i, scalars, state, arrived[i], acc)
        if returned:
            back, returned[-1] = lax.optimization_barrier((back, returned[-1]))
        returned.append(swap(back))
    padded, acc = lax.optimization_barrier((padded, acc))
    near = near_field(near_factor, ends, padded)
    return finish(jnp.concatenate(asked), near, acc, returned)


def solution(mesh):
    placed = (
        P(None, AXES),
        P(None, AXES),
        P(AXES),
        P(),
        P(AXES, None),
        P(AXES),
        P(AXES),
        P(AXES),
    )
    return jax.shard_map(
        local,
        mesh=mesh,
        in_specs=placed,
        out_specs=(P(None, AXES), P(None, AXES)),
        check_vma=False,
    )
```
